32 devices in a mesh: dp: 2 (over x), tensor: 4 (over z), section: 4 (over y, core).
Axes of the slice: x: 2, y: 2, z: 4, core: 2. Of those that a mesh axis runs over, the one named last changes fastest.
Arguments:
- grad_parts: bfloat16 [4, 2, 4, 1024, 1024], P('section', 'dp', None, None, 'tensor'), may hold values from -1.5 to 1.5
- first_moment: float32 [4, 4, 1024, 1024], P('section', 'tensor', 'dp'), may hold values from -3 to 3
- second_moment: float32 [4, 4, 1024, 1024], P('section', 'tensor', 'dp'), may hold values from 0.1 to 4
- left_stat: float32 [4, 4, 1024, 1024], P('section', 'tensor', 'dp'), may hold values from -12288 to 184320
- right_stat: float32 [4, 4, 1024, 1024], P('section', 'tensor', 'dp'), may hold values from -12288 to 184320
- left_basis: float32 [4, 4, 1024, 1024], P('section', 'tensor', 'dp'), may hold values from -0.1875 to 0.1875
- right_basis: float32 [4, 4, 1024, 1024], P('section', 'tensor', 'dp'), may hold values from -0.1875 to 0.1875
- gain_grads: float32 [4, 2, 4, 2, 1024], P('section', 'dp', 'tensor'), may hold values from -1.2 to 1.2
- gain_first: float32 [4, 2, 1024], P('section'), may hold values from -3 to 3
- gain_second: float32 [4, 2, 1024], P('section'), may hold values from 0.1 to 4
- table_grads: float32 [4, 2, 32, 16], P('section', 'dp', None, 'tensor'), may hold values from -1.2 to 1.2
- table_first: float32 [32, 16], P(None, 'tensor'), may hold values from -3 to 3
- table_second: float32 [32, 16], P(None, 'tensor'), may hold values from 0.1 to 4
Outputs:
- update: float32 [4, 4, 1024, 1024], P('section', 'tensor', 'dp')
- first_next: float32 [4, 4, 1024, 1024], P('section', 'tensor', 'dp')
- second_next: float32 [4, 4, 1024, 1024], P('section', 'tensor', 'dp')
- left_next: float32 [4, 4, 1024, 1024], P('section', 'tensor', 'dp')
- right_next: float32 [4, 4, 1024, 1024], P('section', 'tensor', 'dp')
- left_rotation: float32 [4, 4, 1024, 1024], P('section', 'tensor', 'dp')
- right_rotation: float32 [4, 4, 1024, 1024], P('section', 'tensor', 'dp')
- gain_update: float32 [4, 2, 1024], P('section')
- gain_moment: float32 [4, 2, 1024], P('section')
- gain_squares: float32 [4, 2, 1024], P('section')
- table_update: float32 [32, 16], P(None, 'tensor')
- table_moment: float32 [32, 16], P(None, 'tensor')
- table_squares: float32 [32, 16], P(None, 'tensor')
The draws below stay inside these ranges and needn't reach their ends.
All inputs are finite; a program needn't handle non-finite values.
Results may differ from the reference program's by a relative error of at most 0.014.
Values may be sent and summed in bfloat16 or wider, within the bound.
No kernel may reach another device: no remote copies, remote signals or barrier semaphores. Data moves between devices by JAX's collectives and lax.ppermute only.
A program may use at most 128 MiB of HBM per device.

```python
import math
import jax
import jax.numpy as jnp
from jax import lax

D = 1024
HEADS = 16
BUCKETS = 32
MATS = 4
NORMS = 2
NS_ITERS = 3
LAYERS = 4
N_DP = 2
N_TENSOR = 4


def order_of(subkey):
    return jax.random.permutation(subkey, D)


def statistic(key):
    first_key, second_key, third_key = jax.random.split(key, 3)
    base = jax.random.uniform(first_key, (LAYERS, MATS, D, D), jnp.float32, -1.7, 1.7)
    symmetric = 0.5 * (base + jnp.swapaxes(base, -1, -2))
    factor = jax.random.uniform(second_key, (LAYERS, MATS, D), jnp.float32, 1.0, 1.5)
    order_keys = jax.random.split(third_key, LAYERS * MATS)
    ranks = jax.vmap(order_of)(order_keys).reshape(LAYERS, MATS, D)
    scales = factor / jnp.sqrt(ranks.astype(jnp.float32) + 1.0)
    identity = (jnp.arange(D)[:, None] == jnp.arange(D)[None, :]).astype(jnp.float32)
    inner = symmetric * (1.4 / math.sqrt(D)) + 3.0 * identity
    return inner * scales[..., :, None] * scales[..., None, :] * (24.0 * D)


def draw_left_stat(key, part):
    return statistic(jax.random.fold_in(key, 11))


def draw_right_stat(key, part):
    return statistic(jax.random.fold_in(key, 23))


def with_spikes(values, rng, source, target, blocks, factor):
    owner, partner = [(jnp.arange(values.shape[dim]) // (values.shape[dim] // blocks)).reshape([-1 if axis == dim else 1 for axis in range(values.ndim)]) for dim in (source, target)]
    chosen = jax.random.permutation(rng, blocks)[partner]
    strong = (owner == chosen) | (owner == (partner + blocks // 2) % blocks)
    return jnp.where(strong, factor * values, values)


def block_levels(key, dims, cuts, least, top_value):
    loudness = 1.0
    for dim, parts in cuts:
        steps = jax.random.uniform(jax.random.fold_in(jax.random.fold_in(key, 6), dim), (parts,), jnp.float32, least / len(cuts), top_value / len(cuts))
        loudness = loudness * jnp.repeat(jnp.exp(steps), dims[dim] // parts).reshape((-1,) + (1,) * (len(dims) - 1 - dim))
    return loudness


def normal_values(rng, extent, deviation, most, pieces=(), kind=jnp.bfloat16):
    array = jax.random.normal(rng, extent, jnp.float32) * deviation
    if len(pieces) > 0:
        array = block_levels(rng, extent, pieces, -0.22, 0.18) * array
    return jnp.clip(array, min=-most, max=most).astype(kind)


def noise_with(own_key, extent, scale, bound, shards, heavy, kind=jnp.bfloat16):
    drawn = scale * jax.random.normal(own_key, extent, jnp.float32)
    if shards:
        drawn = drawn * block_levels(own_key, extent, shards, -0.22, 0.18)
    return jnp.clip(with_spikes(drawn, jax.random.fold_in(own_key, 3), *heavy), -bound, bound).astype(kind)


def setup_inputs(seed: int = 0) -> dict:
    seeds = jax.random.split(jax.random.key(seed), 14)
    return {
        "grad_parts": noise_with(seeds[0], (LAYERS, N_DP, MATS, D, D), 0.25, 1.5, ((0, 4), (1, 2), (4, 4)), (1, 3, 2, 2.0)),
        "first_moment": normal_values(seeds[1], (LAYERS, MATS, D, D), 0.5, 3.0, ((0, 4), (1, 4), (2, 2)), jnp.float32),
        "second_moment": jnp.clip(jnp.exp(math.log(4.0) - 3.6888794 * jax.random.uniform(seeds[2], (LAYERS, MATS, D, D), jnp.float32) ** block_levels(seeds[2], (LAYERS, MATS, D, D), ((0, 4), (1, 4), (2, 2)), -0.2, 0.2)), 0.1, 4.0),
        "left_stat": draw_left_stat(jax.random.fold_in(seeds[13], 71), 0),
        "right_stat": draw_right_stat(jax.random.fold_in(seeds[13], 71), 0),
        "left_basis": normal_values(seeds[5], (LAYERS, MATS, D, D), D ** -0.5, 0.1875, ((0, 4), (1, 4), (2, 2)), jnp.float32),
        "right_basis": normal_values(seeds[6], (LAYERS, MATS, D, D), D ** -0.5, 0.1875, ((0, 4), (1, 4), (2, 2)), jnp.float32),
        "gain_grads": normal_values(seeds[7], (LAYERS, N_DP, N_TENSOR, NORMS, D), 0.2, 1.2, ((0, 4), (1, 2), (2, 4)), jnp.float32),
        "gain_first": normal_values(seeds[8], (LAYERS, NORMS, D), 0.5, 3.0, ((0, 4),), jnp.float32),
        "gain_second": jnp.clip(jnp.exp(math.log(4.0) - 3.6888794 * jax.random.uniform(seeds[9], (LAYERS, NORMS, D), jnp.float32) ** block_levels(seeds[9], (LAYERS, NORMS, D), ((0, 4),), -0.2, 0.2)), 0.1, 4.0),
        "table_grads": normal_values(seeds[10], (LAYERS, N_DP, BUCKETS, HEADS), 0.2, 1.2, ((0, 4), (1, 2), (3, 4)), jnp.float32),
        "table_first": normal_values(seeds[11], (BUCKETS, HEADS), 0.5, 3.0, ((1, 4),), jnp.float32),
        "table_second": jnp.clip(jnp.exp(math.log(4.0) - 3.6888794 * jax.random.uniform(seeds[12], (BUCKETS, HEADS), jnp.float32) ** block_levels(seeds[12], (BUCKETS, HEADS), ((1, 4),), -0.2, 0.2)), 0.1, 4.0),
    }


beta_first = 0.9
beta_second = 0.95
beta_stat = 0.95
adam_eps = 1e-08
norm_eps = 1e-06
step_count = 10.0

def product(left, right):
    return jnp.dot(left, right, preferred_element_type=jnp.float32)

def to_half(value):
    return value.astype(jnp.bfloat16)

def adam_direction(first, second):
    first_hat = first / (1.0 - beta_first ** step_count)
    second_hat = second / (1.0 - beta_second ** step_count)
    return first_hat / (jnp.sqrt(second_hat) + adam_eps)

def orthogonalize(power):
    iterate = power / jnp.sqrt(jnp.sum(power * power) + norm_eps)
    for sweep in range(NS_ITERS):
        iterate_half = to_half(iterate)
        gram = to_half(product(iterate_half, iterate_half.T))
        iterate = 1.5 * iterate - 0.5 * product(gram, iterate_half)
    return iterate

def reference(grad_parts, first_moment, second_moment, left_stat, right_stat, left_basis, right_basis, gain_grads, gain_first, gain_second, table_grads, table_first, table_second):

    def one_matrix(index):
        layer = index // MATS
        which = index % MATS
        grad_half = to_half(lax.optimization_barrier(jnp.sum(grad_parts[layer, :, which].astype(jnp.float32), axis=0)))
        left_half = to_half(left_basis[layer, which])
        right_half = to_half(right_basis[layer, which])
        rotated_half = to_half(product(grad_half, right_half))
        rotated = product(left_half.T, rotated_half)
        first_new = beta_first * first_moment[layer, which] + (1.0 - beta_first) * rotated
        second_new = beta_second * second_moment[layer, which] + (1.0 - beta_second) * rotated * rotated
        direction = to_half(adam_direction(first_new, second_new))
        back_half = to_half(product(left_half, direction))
        update = product(back_half, right_half.T)
        left_new = beta_stat * left_stat[layer, which] + product(grad_half, grad_half.T)
        right_new = beta_stat * right_stat[layer, which] + product(grad_half.T, grad_half)
        left_rotation = orthogonalize(product(to_half(left_new), left_half))
        right_rotation = orthogonalize(product(to_half(right_new), right_half))
        return (update, first_new, second_new, left_new, right_new, left_rotation, right_rotation)
    results = lax.map(one_matrix, jnp.arange(LAYERS * MATS, dtype=jnp.int32))
    shaped = [item.reshape(LAYERS, MATS, D, D) for item in results]
    gain_sum = lax.optimization_barrier(jnp.sum(gain_grads, axis=(1, 2)))
    gain_moment = beta_first * gain_first + (1.0 - beta_first) * gain_sum
    gain_squares = beta_second * gain_second + (1.0 - beta_second) * gain_sum * gain_sum
    gain_update = adam_direction(gain_moment, gain_squares)
    table_sum = lax.optimization_barrier(jnp.sum(table_grads, axis=(0, 1)))
    table_moment = beta_first * table_first + (1.0 - beta_first) * table_sum
    table_squares = beta_second * table_second + (1.0 - beta_second) * table_sum * table_sum
    table_update = adam_direction(table_moment, table_squares)
    return (shaped[0], shaped[1], shaped[2], shaped[3], shaped[4], shaped[5], shaped[6], gain_update, gain_moment, gain_squares, table_update, table_moment, table_squares)
```

```python
import functools

import jax
import jax.numpy as jnp
from jax import lax
from jax.experimental import pallas as pl
from jax.experimental.pallas import tpu as pltpu
from jax.sharding import PartitionSpec as P

NS_ITERS = 3

beta_first = 0.9
beta_second = 0.95
beta_stat = 0.95
adam_eps = 1e-08
norm_eps = 1e-06
step_count = 10.0

f32 = jnp.float32
bf16 = jnp.bfloat16
MIB = 1024 * 1024

NN = (((1,), (0,)), ((), ()))
NT = (((1,), (1,)), ((), ()))
TN = (((0,), (0,)), ((), ()))


def product(left, right, dims=NN):
    return lax.dot_general(left, right, dims, preferred_element_type=f32)


def adam_direction(first, second):
    first_hat = first / (1.0 - beta_first**step_count)
    second_hat = second / (1.0 - beta_second**step_count)
    return first_hat / (jnp.sqrt(second_hat) + adam_eps)


def tiles(extent, most=256):
    size = min(extent, most)
    return [slice(start, start + size) for start in range(0, extent, size)]


def join(whole, offsets, pieces):
    for place, piece in enumerate(pieces):
        count = piece.shape[0]
        whole[pl.ds(pl.multiple_of(offsets[place], count), count), :] = piece[...]


def call(kernel, outs, scratch, flops, nbytes, *operands):
    return pl.pallas_call(
        kernel,
        out_shape=outs,
        in_specs=[pl.BlockSpec(memory_space=pltpu.SMEM)]
        + [pl.BlockSpec(memory_space=pltpu.VMEM)] * (len(operands) - 1),
        out_specs=[pl.BlockSpec(memory_space=pltpu.VMEM)] * len(outs),
        scratch_shapes=scratch,
        compiler_params=pltpu.CompilerParams(vmem_limit_bytes=40 * MIB),
    )(*operands)


def shape(rows, columns, dtype):
    return jax.ShapeDtypeStruct((rows, columns), dtype)


def assemble_kernel(width, places, *refs):
    *blocks, out = refs
    for place, block in enumerate(blocks):
        out[:, pl.ds(pl.multiple_of(places[place], width), width)] = block[...]


def stats_kernel(n, offsets, *refs):
    pieces, column_pieces = refs[:n], refs[n : 2 * n]
    rows_ref, left_stat, right_stat = refs[2 * n : 2 * n + 3]
    left_next, left_half, right_next, right_half, grad, columns = refs[2 * n + 3 :]
    join(grad, offsets, pieces)
    join(columns, offsets, column_pieces)
    for at in tiles(rows_ref.shape[0]):
        value = beta_stat * left_stat[at] + product(rows_ref[at], grad[...], NT)
        left_next[at] = value
        left_half[at] = value.astype(bf16)
    for at in tiles(rows_ref.shape[0]):
        value = beta_stat * right_stat[at] + product(columns[:, at], grad[...], TN)
        right_next[at] = value
        right_half[at] = value.astype(bf16)


def moments_kernel(n, nr, offsets, *refs):
    pieces, column_pieces, right_pieces = refs[:n], refs[n : 2 * n], refs[2 * n : 2 * n + nr]
    first, second = refs[2 * n + nr : 2 * n + nr + 2]
    first_next, second_next, direction, grad, columns, right, rotated_half = refs[2 * n + nr + 2 :]
    join(grad, [offsets[i] for i in range(n)], pieces)
    join(columns, [offsets[i] for i in range(n)], column_pieces)
    join(right, [offsets[n + i] for i in range(nr)], right_pieces)
    for at in tiles(grad.shape[0]):
        rotated_half[at] = product(grad[at], right[...]).astype(bf16)
    for at in tiles(first.shape[0]):
        rotated = product(columns[:, at], rotated_half[...], TN)
        first_new = beta_first * first[at] + (1.0 - beta_first) * rotated
        second_new = beta_second * second[at] + (1.0 - beta_second) * rotated * rotated
        first_next[at] = first_new
        second_next[at] = second_new
        direction[at] = adam_direction(first_new, second_new).astype(bf16)


def update_kernel(n, nr, offsets, *refs):
    pieces, right_pieces, rows_ref = refs[:n], refs[n : n + nr], refs[n + nr]
    update, direction, right = refs[n + nr + 1 :]
    join(direction, [offsets[i] for i in range(n)], pieces)
    join(right, [offsets[n + i] for i in range(nr)], right_pieces)
    for at in tiles(rows_ref.shape[0]):
        back_half = product(rows_ref[at], direction[...]).astype(bf16)
        update[at] = product(back_half, right[...], NT)


def rotation_kernel(ns, nb, offsets, *refs):
    stat_pieces, basis_pieces = refs[:ns], refs[ns : ns + nb]
    out, stat, basis, iterate, half_a, half_b = refs[ns + nb :]
    rows = out.shape[0]
    extent = stat.shape[0]
    join(stat, [offsets[i] for i in range(ns)], stat_pieces)
    join(basis, [offsets[ns + i] for i in range(nb)], basis_pieces)
    size = min(extent, 256)

    def at(step, base=0):
        return pl.ds(pl.multiple_of(base + step * size, size), size)

    def power_tile(step, total):
        power = product(stat[at(step), :], basis[...])
        iterate[at(step), :] = power
        return total + jnp.sum(power * power)

    squares = lax.fori_loop(0, extent // size, power_tile, jnp.zeros((), f32))
    scale = 1.0 / jnp.sqrt(squares + norm_eps)

    def scale_tile(step, carry):
        value = iterate[at(step), :] * scale
        iterate[at(step), :] = value
        half_a[at(step), :] = value.astype(bf16)
        return carry

    lax.fori_loop(0, extent // size, scale_tile, 0)
    halves = (half_a, half_b)
    for sweep in range(NS_ITERS):
        source, target = halves[sweep % 2], halves[(sweep + 1) % 2]
        if sweep < NS_ITERS - 1:

            def sweep_tile(step, carry, source=source, target=target):
                gram = product(source[at(step), :], source[...], NT).astype(bf16)
                value = 1.5 * iterate[at(step), :] - 0.5 * product(gram, source[...])
                iterate[at(step), :] = value
                target[at(step), :] = value.astype(bf16)
                return carry

            lax.fori_loop(0, extent // size, sweep_tile, 0)
        else:
            own = min(rows, size)
            base = offsets[ns + nb]

            def last_tile(step, carry, source=source):
                here = pl.ds(pl.multiple_of(base + step * own, own), own)
                gram = product(source[here, :], source[...], NT).astype(bf16)
                value = 1.5 * iterate[here, :] - 0.5 * product(gram, source[...])
                out[pl.ds(pl.multiple_of(step * own, own), own), :] = value
                return carry

            lax.fori_loop(0, rows // own, last_tile, 0)


def build(mesh):
    n_dp, n_tensor, n_section = mesh.shape["dp"], mesh.shape["tensor"], mesh.shape["section"]
    pair = n_dp == 2

    def swap(value):
        return lax.ppermute(value, "dp", [(0, 1), (1, 0)])

    def total(value, axis, count):
        if count & (count - 1):
            return lax.psum(value, axis)
        step = 1
        while step < count:
            value = value + lax.ppermute(value, axis, [(i, i ^ step) for i in range(count)])
            step *= 2
        return value

    def after(value, *others):
        return lax.optimization_barrier((value,) + others)[0]

    def local(
        grad_parts,
        first_moment,
        second_moment,
        left_stat,
        right_stat,
        left_basis,
        right_basis,
        gain_grads,
        gain_first,
        gain_second,
        table_grads,
        table_first,
        table_second,
    ):
        partial_value = grad_parts[0, 0]
        mats, extent, width = partial_value.shape
        rows = left_basis.shape[2]
        dp = lax.axis_index("dp")
        rank = lax.axis_index("tensor")
        own = dp * rows
        other = (n_dp - 1 - dp) * rows

        def rows_of(value, start):
            return lax.dynamic_slice_in_dim(value, start, rows, 1)

        gain_part = gain_grads[0, 0, 0]
        table_part = table_grads[0, 0]
        both = jnp.concatenate([gain_part.reshape(-1), table_part.reshape(-1)])
        both = total(both, "dp", n_dp)

        if pair:
            received = swap(rows_of(partial_value, other))
            received, both = lax.optimization_barrier((received, both))
            left_local = left_basis[0, 0].astype(bf16)
            right_local = right_basis[0, 0].astype(bf16)
            left_other = swap(after(left_local, both))
            summed = (
                rows_of(partial_value, own).astype(f32) + received.astype(f32)
            ).astype(bf16)
            middle = rows // 4
            right_other_a = swap(after(right_local[:middle], summed))
            blocks = []
            places = []
            for step in range(n_tensor):
                block = lax.dynamic_index_in_dim(summed, rank ^ step, 0, keepdims=False)
                if step:
                    block = lax.ppermute(
                        block, "tensor", [(i, i ^ step) for i in range(n_tensor)]
                    )
                blocks.append(block)
                places.append((rank ^ step) * width)
            *blocks, left_other, right_other_a = lax.optimization_barrier(
                (*blocks, left_other, right_other_a)
            )
            (grad_rows,) = call(
                functools.partial(assemble_kernel, width),
                [shape(rows, extent, bf16)],
                [],
                0,
                4 * rows * extent,
                jnp.stack(places),
                *blocks,
            )
            grad_other = swap(grad_rows)
            right_other_b = swap(after(right_local[middle:], grad_rows))
            grad_pieces = [grad_rows, grad_other]
            left_pieces = [left_local, left_other]
            right_pieces = [right_local, right_other_a, right_other_b]
            offsets = jnp.stack([own, other])
            right_offsets = jnp.stack([own, other, other + middle])
        else:
            columns = lax.all_to_all(partial_value, "tensor", split_axis=0, concat_axis=2, tiled=True)
            summed = lax.psum_scatter(columns, "dp", scatter_dimension=1, tiled=True)
            grad_rows = summed[0]
            left_local = left_basis[0, 0].astype(bf16)
            right_local = right_basis[0, 0].astype(bf16)

            def gather(value):
                return [lax.all_gather(value, "dp", axis=0, tiled=True)]

            grad_pieces, left_pieces, right_pieces = (
                gather(grad_rows),
                gather(left_local),
                gather(right_local),
            )
            offsets = right_offsets = jnp.zeros((1,), jnp.int32)
        gain_sum = total(both[: gain_part.size].reshape(gain_part.shape), "tensor", n_tensor)
        table_sum = total(both[gain_part.size :].reshape(table_part.shape), "section", n_section)
        n, nr = len(grad_pieces), len(right_pieces)
        cube = 2 * extent**3

        def columns_of(pieces):
            return [lax.dynamic_slice_in_dim(piece, own, rows, 1) for piece in pieces]

        left_new, left_new_half, right_new, right_new_half = call(
            functools.partial(stats_kernel, n),
            [shape(rows, extent, f32), shape(rows, extent, bf16)] * 2,
            [pltpu.VMEM((extent, extent), bf16), pltpu.VMEM((extent, rows), bf16)],
            cube,
            12 * MIB,
            offsets,
            *grad_pieces,
            *columns_of(grad_pieces),
            grad_rows,
            left_stat[0, 0],
            right_stat[0, 0],
        )
        if pair:
            left_new_pieces = [left_new_half, swap(left_new_half)]
            right_new_pieces = [right_new_half, swap(right_new_half)]
        else:
            left_new_pieces, right_new_pieces = gather(left_new_half), gather(right_new_half)
        first_new, second_new, direction = call(
            functools.partial(moments_kernel, n, nr),
            [shape(rows, extent, f32)] * 2 + [shape(rows, extent, bf16)],
            [
                pltpu.VMEM((extent, extent), bf16),
                pltpu.VMEM((extent, rows), bf16),
                pltpu.VMEM((extent, extent), bf16),
                pltpu.VMEM((extent, extent), bf16),
            ],
            cube * 3 // 2,
            12 * MIB,
            jnp.concatenate([offsets, right_offsets]),
            *grad_pieces,
            *columns_of(left_pieces),
            *right_pieces,
            first_moment[0, 0],
            second_moment[0, 0],
        )
        direction_pieces = [direction, swap(direction)] if pair else gather(direction)

        def rotation(stat_pieces, basis_pieces, basis_offsets):
            return call(
                functools.partial(rotation_kernel, len(stat_pieces), len(basis_pieces)),
                [shape(rows, extent, f32)],
                [
                    pltpu.VMEM((extent, extent), bf16),
                    pltpu.VMEM((extent, extent), bf16),
                    pltpu.VMEM((extent, extent), f32),
                    pltpu.VMEM((extent, extent), bf16),
                    pltpu.VMEM((extent, extent), bf16),
                ],
                cube * 6,
                6 * MIB,
                jnp.concatenate([offsets, basis_offsets, jnp.stack([own])]),
                *stat_pieces,
                *basis_pieces,
            )[0]

        left_new_pieces[-1] = after(left_new_pieces[-1], direction)
        left_rotation = rotation(left_new_pieces, left_pieces, offsets)
        right_new_pieces[-1] = after(right_new_pieces[-1], left_rotation)
        right_rotation = rotation(right_new_pieces, right_pieces, right_offsets)
        direction_pieces[-1] = after(direction_pieces[-1], right_rotation)
        (update,) = call(
            functools.partial(update_kernel, n, nr),
            [shape(rows, extent, f32)],
            [pltpu.VMEM((extent, extent), bf16), pltpu.VMEM((extent, extent), bf16)],
            cube,
            7 * MIB,
            jnp.concatenate([offsets, right_offsets]),
            *direction_pieces,
            *right_pieces,
            left_local,
        )

        gain_moment = beta_first * gain_first[0] + (1.0 - beta_first) * gain_sum
        gain_squares = beta_second * gain_second[0] + (1.0 - beta_second) * gain_sum * gain_sum
        gain_update = adam_direction(gain_moment, gain_squares)
        table_moment = beta_first * table_first + (1.0 - beta_first) * table_sum
        table_squares = beta_second * table_second + (1.0 - beta_second) * table_sum * table_sum
        table_update = adam_direction(table_moment, table_squares)
        return (
            update[None, None],
            first_new[None, None],
            second_new[None, None],
            left_new[None, None],
            right_new[None, None],
            left_rotation[None, None],
            right_rotation[None, None],
            gain_update[None],
            gain_moment[None],
            gain_squares[None],
            table_update,
            table_moment,
            table_squares,
        )

    return local


def solution(mesh):
    state = P("section", "tensor", "dp", None)
    gains = P("section", None, None)
    table = P(None, "tensor")
    return jax.shard_map(
        build(mesh),
        mesh=mesh,
        in_specs=(P("section", "dp", None, None, "tensor"),)
        + (state,) * 6
        + (P("section", "dp", "tensor", None, None), gains, gains)
        + (P("section", "dp", None, "tensor"), table, table),
        out_specs=(state,) * 7 + (gains,) * 3 + (table,) * 3,
        check_vma=False,
    )
```

```python
import functools

import jax
import jax.numpy as jnp
from jax import lax
from jax.experimental import pallas as pl
from jax.experimental.pallas import tpu as pltpu
from jax.sharding import PartitionSpec as P

NS_ITERS = 3

beta_first = 0.9
beta_second = 0.95
beta_stat = 0.95
adam_eps = 1e-08
norm_eps = 1e-06
step_count = 10.0

f32 = jnp.float32
bf16 = jnp.bfloat16
MIB = 1024 * 1024

NN = (((1,), (0,)), ((), ()))
NT = (((1,), (1,)), ((), ()))
TN = (((0,), (0,)), ((), ()))


def product(left, right, dims=NN):
    return lax.dot_general(left, right, dims, preferred_element_type=f32)


def adam_direction(first, second):
    first_hat = first / (1.0 - beta_first**step_count)
    second_hat = second / (1.0 - beta_second**step_count)
    return first_hat / (jnp.sqrt(second_hat) + adam_eps)


def tiles(extent, most=256):
    size = min(extent, most)
    return [slice(start, start + size) for start in range(0, extent, size)]


def join(whole, offsets, pieces):
    for place, piece in enumerate(pieces):
        count = piece.shape[0]
        whole[pl.ds(pl.multiple_of(offsets[place], count), count), :] = piece[...]


def call(kernel, outs, scratch, *operands):
    return pl.pallas_call(
        kernel,
        out_shape=outs,
        in_specs=[pl.BlockSpec(memory_space=pltpu.SMEM)]
        + [pl.BlockSpec(memory_space=pltpu.VMEM)] * (len(operands) - 1),
        out_specs=[pl.BlockSpec(memory_space=pltpu.VMEM)] * len(outs),
        scratch_shapes=scratch,
        compiler_params=pltpu.CompilerParams(vmem_limit_bytes=40 * MIB),
    )(*operands)


def shape(rows, columns, dtype):
    return jax.ShapeDtypeStruct((rows, columns), dtype)


def assemble_kernel(width, places, *refs):
    *blocks, out = refs
    for place, block in enumerate(blocks):
        out[:, pl.ds(pl.multiple_of(places[place], width), width)] = block[...]


def place_kernel(start, side, part, left_in, right_in, left, right, wide, sem):
    del left_in, right_in
    wide[...] = part[...].astype(f32)
    here = pl.ds(start, part.shape[0])

    @pl.when(side[0] == 1)
    def _():
        copy = pltpu.make_async_copy(wide, right.at[here], sem)
        copy.start()
        copy.wait()

    @pl.when(side[0] != 1)
    def _():
        copy = pltpu.make_async_copy(wide, left.at[here], sem)
        copy.start()
        copy.wait()


def place(side, part, start, left, right):
    anywhere = pl.BlockSpec(memory_space=pl.ANY)
    return pl.pallas_call(
        functools.partial(place_kernel, start),
        out_shape=[shape(*left.shape, f32)] * 2,
        in_specs=[
            pl.BlockSpec(memory_space=pltpu.SMEM),
            pl.BlockSpec(memory_space=pltpu.VMEM),
            anywhere,
            anywhere,
        ],
        out_specs=[anywhere, anywhere],
        scratch_shapes=[pltpu.VMEM(part.shape, f32), pltpu.SemaphoreType.DMA],
        input_output_aliases={2: 0, 3: 1},
    )(side, part, left, right)


def basis_kernel(n_left, n_right, offsets, *refs):
    left_pieces, right_pieces = refs[:n_left], refs[n_left : n_left + n_right]
    out = refs[-1]
    left_side = offsets[n_left + n_right] == 1

    @pl.when(left_side)
    def _():
        join(out, [offsets[i] for i in range(n_left)], left_pieces)

    @pl.when(jnp.logical_not(left_side))
    def _():
        join(out, [offsets[n_left + i] for i in range(n_right)], right_pieces)


def stats_kernel(n, offsets, *refs):
    pieces, column_pieces = refs[:n], refs[n : 2 * n]
    rows_ref, left_stat, right_stat = refs[2 * n : 2 * n + 3]
    left_next, right_next, keep, send, grad, columns = refs[2 * n + 3 :]
    join(grad, offsets, pieces)
    join(columns, offsets, column_pieces)
    for at in tiles(rows_ref.shape[0]):
        left_next[at] = beta_stat * left_stat[at] + product(rows_ref[at], grad[...], NT)
    for at in tiles(rows_ref.shape[0]):
        right_next[at] = beta_stat * right_stat[at] + product(columns[:, at], grad[...], TN)
    left_side = offsets[n] == 1

    @pl.when(left_side)
    def _():
        keep[...] = left_next[...].astype(bf16)
        send[...] = right_next[...].astype(bf16)

    @pl.when(jnp.logical_not(left_side))
    def _():
        keep[...] = right_next[...].astype(bf16)
        send[...] = left_next[...].astype(bf16)


def moments_kernel(n, offsets, *refs):
    pieces, column_pieces, right_pieces = refs[:n], refs[n : 2 * n], refs[2 * n : 3 * n]
    first, second = refs[3 * n : 3 * n + 2]
    first_next, second_next, direction, grad, columns, right, rotated_half = refs[3 * n + 2 :]
    join(grad, offsets, pieces)
    join(columns, offsets, column_pieces)
    join(right, offsets, right_pieces)
    for at in tiles(grad.shape[0]):
        rotated_half[at] = product(grad[at], right[...]).astype(bf16)
    for at in tiles(first.shape[0]):
        rotated = product(columns[:, at], rotated_half[...], TN)
        first_new = beta_first * first[at] + (1.0 - beta_first) * rotated
        second_new = beta_second * second[at] + (1.0 - beta_second) * rotated * rotated
        first_next[at] = first_new
        second_next[at] = second_new
        direction[at] = adam_direction(first_new, second_new).astype(bf16)


def update_kernel(n, offsets, *refs):
    pieces, right_pieces, rows_ref = refs[:n], refs[n : 2 * n], refs[2 * n]
    update, direction, right = refs[2 * n + 1 :]
    join(direction, offsets, pieces)
    join(right, offsets, right_pieces)
    for at in tiles(rows_ref.shape[0]):
        back_half = product(rows_ref[at], direction[...]).astype(bf16)
        update[at] = product(back_half, right[...], NT)


def rotation_kernel(ns, n_out, offsets, *refs):
    stat_pieces, basis, outs = refs[:ns], refs[ns], refs[ns + 1 : ns + 1 + n_out]
    stat, iterate, half_a, half_b = refs[ns + 1 + n_out :]
    join(stat, offsets, stat_pieces)
    squares = jnp.zeros((), f32)
    for at in tiles(stat.shape[0]):
        power = product(stat[at], basis[...])
        iterate[at] = power
        squares += jnp.sum(power * power)
    scale = 1.0 / jnp.sqrt(squares + norm_eps)
    for at in tiles(stat.shape[0]):
        value = iterate[at] * scale
        iterate[at] = value
        half_a[at] = value.astype(bf16)

    def step(source, at):
        gram = product(source[at], source[...], NT).astype(bf16)
        return 1.5 * iterate[at] - 0.5 * product(gram, source[...])

    source, target = half_a, half_b
    for sweep in range(NS_ITERS - 1):
        for at in tiles(stat.shape[0]):
            value = step(source, at)
            iterate[at] = value
            target[at] = value.astype(bf16)
        source, target = target, source
    for place, out in enumerate(outs):
        for at in tiles(out.shape[0]):
            size = at.stop - at.start
            here = pl.ds(pl.multiple_of(offsets[ns + place] + at.start, size), size)
            out[at] = step(source, here).astype(out.dtype)


def build(mesh):
    n_dp, n_tensor, n_section = mesh.shape["dp"], mesh.shape["tensor"], mesh.shape["section"]
    pair = n_dp == 2

    def swap(value):
        return lax.ppermute(value, "dp", [(0, 1), (1, 0)])

    def total(value, axis, count):
        if count & (count - 1):
            return lax.psum(value, axis)
        step = 1
        while step < count:
            value = value + lax.ppermute(value, axis, [(i, i ^ step) for i in range(count)])
            step *= 2
        return value

    def after(value, *others):
        return lax.optimization_barrier((value,) + others)[0]

    def local(
        grad_parts,
        first_moment,
        second_moment,
        left_stat,
        right_stat,
        left_basis,
        right_basis,
        gain_grads,
        gain_first,
        gain_second,
        table_grads,
        table_first,
        table_second,
    ):
        partial_value = grad_parts[0, 0]
        mats, extent, width = partial_value.shape
        rows = left_basis.shape[2]
        dp = lax.axis_index("dp")
        rank = lax.axis_index("tensor")
        own = dp * rows
        other = (n_dp - 1 - dp) * rows

        def columns_of(pieces):
            return [lax.dynamic_slice_in_dim(piece, own, rows, 1) for piece in pieces]

        gain_part = gain_grads[0, 0, 0]
        table_part = table_grads[0, 0]
        both = jnp.concatenate([gain_part.reshape(-1), table_part.reshape(-1)])
        both = total(both, "dp", n_dp)

        if pair:
            section = lax.axis_index("section")
            left_side = (dp == section % 2).astype(jnp.int32)
            left_local = left_basis[0, 0].astype(bf16)
            right_local = right_basis[0, 0].astype(bf16)
            last = None
            blocks = [None] * n_tensor
            for step in reversed(range(n_tensor)):
                mine = lax.dynamic_index_in_dim(partial_value, rank ^ step, 0, keepdims=False)
                sent = lax.dynamic_slice_in_dim(mine, other, rows, 0)
                got = swap(sent)
                if last is None:
                    left_local_out = after(left_local, got)
                else:
                    got = after(got, last)
                block = lax.dynamic_slice_in_dim(mine, own, rows, 0).astype(f32) + got.astype(f32)
                last = block = block.astype(bf16)
                if step:
                    block = lax.ppermute(
                        block, "tensor", [(i, i ^ step) for i in range(n_tensor)]
                    )
                blocks[step] = block
            left_cross_out = lax.dynamic_slice_in_dim(left_local_out, other, rows, 1)
            left_cross = swap(left_cross_out)
            left_rest = lax.ppermute(
                lax.dynamic_slice_in_dim(left_local_out, own, rows, 1),
                ("dp", "section"),
                [
                    ((1 - s % 2) * n_section + s, (s % 2) * n_section + s)
                    for s in range(n_section)
                ],
            )
            head = rows // 4
            right_head = swap(after(right_local[:head], last))
            places = jnp.stack([(rank ^ step) * width for step in range(n_tensor)])
            *blocks, both, left_cross, left_rest = lax.optimization_barrier(
                (*blocks, both, left_cross, left_rest)
            )
            (grad_rows,) = call(
                functools.partial(assemble_kernel, width),
                [shape(rows, extent, bf16)],
                [],
                places,
                *blocks,
            )
            grad_other, right_head = lax.optimization_barrier((swap(grad_rows), right_head))
            right_other = jnp.concatenate(
                [right_head, swap(after(right_local[head:], grad_rows))], axis=0
            )
            grad_pieces = [grad_rows, grad_other]
            right_pieces = [right_local, right_other]
            offsets = jnp.stack([own, other])
            left_columns = [lax.dynamic_slice_in_dim(left_local, own, rows, 1), left_cross]
        else:
            columns = lax.all_to_all(partial_value, "tensor", split_axis=0, concat_axis=2, tiled=True)
            summed = lax.psum_scatter(columns, "dp", scatter_dimension=1, tiled=True)
            grad_rows = summed[0]
            left_local = left_basis[0, 0].astype(bf16)
            right_local = right_basis[0, 0].astype(bf16)

            def gather(value):
                return [lax.all_gather(value, "dp", axis=0, tiled=True)]

            grad_pieces, left_pieces, right_pieces = (
                gather(grad_rows),
                gather(left_local),
                gather(right_local),
            )
            offsets = jnp.zeros((1,), jnp.int32)
            left_columns = columns_of(left_pieces)
            left_side = jnp.int32(1)
        gain_sum = total(both[: gain_part.size].reshape(gain_part.shape), "tensor", n_tensor)
        table_sum = total(both[gain_part.size :].reshape(table_part.shape), "section", n_section)
        grad_pieces[-1], gain_sum, table_sum = lax.optimization_barrier(
            (grad_pieces[-1], gain_sum, table_sum)
        )
        n = len(grad_pieces)
        square = pltpu.VMEM((extent, extent), bf16)
        strip = pltpu.VMEM((extent, rows), bf16)

        left_new, right_new, stat_keep, stat_send = call(
            functools.partial(stats_kernel, n),
            [shape(rows, extent, f32)] * 2 + [shape(rows, extent, bf16)] * 2,
            [square, strip],
            jnp.concatenate([offsets, left_side[None]]),
            *grad_pieces,
            *columns_of(grad_pieces),
            grad_rows,
            left_stat[0, 0],
            right_stat[0, 0],
        )
        stat_other = swap(stat_send) if pair else None
        first_new, second_new, direction = call(
            functools.partial(moments_kernel, n),
            [shape(rows, extent, f32)] * 2 + [shape(rows, extent, bf16)],
            [square, strip, square, square],
            offsets,
            *grad_pieces,
            *left_columns,
            *right_pieces,
            first_moment[0, 0],
            second_moment[0, 0],
        )
        direction_pieces = [direction, swap(direction)] if pair else gather(direction)

        def rotation(stat_pieces, basis, outs, bases):
            return call(
                functools.partial(rotation_kernel, len(stat_pieces), len(outs)),
                outs,
                [square, pltpu.VMEM((extent, extent), f32), square, square],
                jnp.concatenate([offsets, jnp.stack(bases)]),
                *stat_pieces,
                basis,
            )

        own_rows = shape(rows, extent, f32)
        if pair:
            left_other = jnp.where(
                own < rows,
                jnp.concatenate([left_cross, left_rest], axis=1),
                jnp.concatenate([left_rest, left_cross], axis=1),
            )
            (basis,) = call(
                functools.partial(basis_kernel, n, n),
                [shape(extent, extent, bf16)],
                [],
                jnp.concatenate([offsets, offsets, left_side[None]]),
                left_local,
                left_other,
                *right_pieces,
            )
            basis = after(basis, direction)
            rotation_own, rotation_send = rotation(
                [stat_keep, stat_other],
                basis,
                [own_rows, shape(rows, extent, bf16)],
                [own, other],
            )
            direction_pieces[1] = after(direction_pieces[1], rotation_send)
            cut = rows * 3 // 4
            rotation_parts = [swap(rotation_send[:cut])]
            rotation_parts.append(swap(rotation_send[cut:]))
            left_rotation, right_rotation = rotation_own, rotation_own
        else:
            (left_rotation,) = rotation(gather(stat_keep), left_pieces[0], [own_rows], [own])
            (right_rotation,) = rotation(gather(stat_send), right_pieces[0], [own_rows], [own])
        (update,) = call(
            functools.partial(update_kernel, n),
            [own_rows],
            [square, square],
            offsets,
            *direction_pieces,
            *right_pieces,
            left_local,
        )
        if pair:
            rotation_parts[0] = after(rotation_parts[0], update)
            for start, part in zip((0, cut), rotation_parts):
                left_rotation, right_rotation = place(
                    left_side[None], part, start, left_rotation, right_rotation
                )

        gain_moment = beta_first * gain_first[0] + (1.0 - beta_first) * gain_sum
        gain_squares = beta_second * gain_second[0] + (1.0 - beta_second) * gain_sum * gain_sum
        gain_update = adam_direction(gain_moment, gain_squares)
        table_moment = beta_first * table_first + (1.0 - beta_first) * table_sum
        table_squares = beta_second * table_second + (1.0 - beta_second) * table_sum * table_sum
        table_update = adam_direction(table_moment, table_squares)
        return (
            update[None, None],
            first_new[None, None],
            second_new[None, None],
            left_new[None, None],
            right_new[None, None],
            left_rotation[None, None],
            right_rotation[None, None],
            gain_update[None],
            gain_moment[None],
            gain_squares[None],
            table_update,
            table_moment,
            table_squares,
        )

    return local


def solution(mesh):
    state = P("section", "tensor", "dp", None)
    gains = P("section", None, None)
    table = P(None, "tensor")
    return jax.shard_map(
        build(mesh),
        mesh=mesh,
        in_specs=(P("section", "dp", None, None, "tensor"),)
        + (state,) * 6
        + (P("section", "dp", "tensor", None, None), gains, gains)
        + (P("section", "dp", None, "tensor"), table, table),
        out_specs=(state,) * 7 + (gains,) * 3 + (table,) * 3,
        check_vma=False,
    )
```

```python
import functools

import jax
import jax.numpy as jnp
from jax import lax
from jax.experimental import pallas as pl
from jax.experimental.pallas import tpu as pltpu
from jax.sharding import PartitionSpec as P

NS_ITERS = 3

beta_first = 0.9
beta_second = 0.95
beta_stat = 0.95
adam_eps = 1e-08
norm_eps = 1e-06
step_count = 10.0

f32 = jnp.float32
bf16 = jnp.bfloat16
MIB = 1024 * 1024

NN = (((1,), (0,)), ((), ()))
NT = (((1,), (1,)), ((), ()))
TN = (((0,), (0,)), ((), ()))


def product(left, right, dims=NN):
    return lax.dot_general(left, right, dims, preferred_element_type=f32)


def adam_direction(first, second):
    first_hat = first / (1.0 - beta_first**step_count)
    second_hat = second / (1.0 - beta_second**step_count)
    return first_hat / (jnp.sqrt(second_hat) + adam_eps)


def tiles(extent, most=256):
    size = min(extent, most)
    return [slice(start, start + size) for start in range(0, extent, size)]


def join(whole, offsets, pieces):
    for place, piece in enumerate(pieces):
        count = piece.shape[0]
        whole[pl.ds(pl.multiple_of(offsets[place], count), count), :] = piece[...]


def call(kernel, outs, scratch, *operands):
    return pl.pallas_call(
        kernel,
        out_shape=outs,
        in_specs=[pl.BlockSpec(memory_space=pltpu.SMEM)]
        + [pl.BlockSpec(memory_space=pltpu.VMEM)] * (len(operands) - 1),
        out_specs=[pl.BlockSpec(memory_space=pltpu.VMEM)] * len(outs),
        scratch_shapes=scratch,
        compiler_params=pltpu.CompilerParams(vmem_limit_bytes=40 * MIB),
    )(*operands)


def shape(rows, columns, dtype):
    return jax.ShapeDtypeStruct((rows, columns), dtype)


def assemble_kernel(width, places, *refs):
    *blocks, out = refs
    for place, block in enumerate(blocks):
        out[:, pl.ds(pl.multiple_of(places[place], width), width)] = block[...]


def place_kernel(start, side, part, left_in, right_in, left, right, wide, sem):
    del left_in, right_in
    wide[...] = part[...].astype(f32)
    here = pl.ds(start, part.shape[0])

    @pl.when(side[0] == 1)
    def _():
        copy = pltpu.make_async_copy(wide, right.at[here], sem)
        copy.start()
        copy.wait()

    @pl.when(side[0] != 1)
    def _():
        copy = pltpu.make_async_copy(wide, left.at[here], sem)
        copy.start()
        copy.wait()


def place(side, part, start, left, right):
    anywhere = pl.BlockSpec(memory_space=pl.ANY)
    return pl.pallas_call(
        functools.partial(place_kernel, start),
        out_shape=[shape(*left.shape, f32)] * 2,
        in_specs=[
            pl.BlockSpec(memory_space=pltpu.SMEM),
            pl.BlockSpec(memory_space=pltpu.VMEM),
            anywhere,
            anywhere,
        ],
        out_specs=[anywhere, anywhere],
        scratch_shapes=[pltpu.VMEM(part.shape, f32), pltpu.SemaphoreType.DMA],
        input_output_aliases={2: 0, 3: 1},
    )(side, part, left, right)


def join_kernel(offsets, *refs):
    *pieces, out = refs
    join(out, offsets, pieces)


def basis_kernel(n, scalars, *refs):
    *left_pieces, right, out = refs
    left_side = scalars[n] == 1

    @pl.when(left_side)
    def _():
        join(out, scalars, left_pieces)

    @pl.when(jnp.logical_not(left_side))
    def _():
        out[...] = right[...]


def stats_kernel(n, offsets, *refs):
    pieces, column_pieces = refs[:n], refs[n : 2 * n]
    rows_ref, left_stat, right_stat = refs[2 * n : 2 * n + 3]
    left_next, right_next, left_half, right_half, grad, columns = refs[2 * n + 3 :]
    join(grad, offsets, pieces)
    join(columns, offsets, column_pieces)
    for at in tiles(rows_ref.shape[0]):
        left_new = beta_stat * left_stat[at] + product(rows_ref[at], grad[...], NT)
        right_new = beta_stat * right_stat[at] + product(columns[:, at], grad[...], TN)
        left_next[at] = left_new
        right_next[at] = right_new
        left_half[at] = left_new.astype(bf16)
        right_half[at] = right_new.astype(bf16)


def pair_stats_kernel(offsets, *refs):
    (own_rows, other_rows), left_stat, right_stat = refs[:2], refs[2], refs[3]
    left_next, right_next, keep, added, grad = refs[4:]
    join(grad, offsets, (own_rows, other_rows))
    count = own_rows.shape[0]
    own = pl.multiple_of(offsets[0], count)
    other = pl.multiple_of(offsets[1], count)
    for at in tiles(count):
        columns = grad[:, pl.ds(own + at.start, at.stop - at.start)]
        left_next[at] = beta_stat * left_stat[at] + product(own_rows[at], grad[...], NT)
        right_next[at] = beta_stat * right_stat[at] + product(columns, grad[...], TN)
    left_side = offsets[2] == 1

    @pl.when(left_side)
    def _():
        keep[...] = left_next[...].astype(bf16)
        for at in tiles(count):
            added[at] = product(other_rows[at], grad[...], NT)

    @pl.when(jnp.logical_not(left_side))
    def _():
        keep[...] = right_next[...].astype(bf16)
        for at in tiles(count):
            columns = grad[:, pl.ds(other + at.start, at.stop - at.start)]
            added[at] = product(columns, grad[...], TN)


def moments_kernel(n, offsets, *refs):
    pieces, column_pieces, right = refs[:n], refs[n : 2 * n], refs[2 * n]
    first, second = refs[2 * n + 1 : 2 * n + 3]
    first_next, second_next, direction, grad, columns, rotated_half = refs[2 * n + 3 :]
    join(grad, offsets, pieces)
    join(columns, offsets, column_pieces)
    for at in tiles(grad.shape[0]):
        rotated_half[at] = product(grad[at], right[...]).astype(bf16)
    for at in tiles(first.shape[0]):
        rotated = product(columns[:, at], rotated_half[...], TN)
        first_new = beta_first * first[at] + (1.0 - beta_first) * rotated
        second_new = beta_second * second[at] + (1.0 - beta_second) * rotated * rotated
        first_next[at] = first_new
        second_next[at] = second_new
        direction[at] = adam_direction(first_new, second_new).astype(bf16)


def update_kernel(n, offsets, *refs):
    pieces, right, rows_ref, update, direction = refs[:n], *refs[n:]
    join(direction, offsets, pieces)
    for at in tiles(rows_ref.shape[0]):
        back_half = product(rows_ref[at], direction[...]).astype(bf16)
        update[at] = product(back_half, right[...], NT)


def rotation_kernel(ns, n_out, offsets, *refs):
    stat_pieces, basis, outs = refs[:ns], refs[ns], refs[-4 - n_out : -4]
    stat, iterate, half_a, half_b = refs[-4:]
    join(stat, offsets, stat_pieces[:1])
    if ns > 1:
        before, added = stat_pieces[1], refs[ns + 1]
        count = before.shape[0]
        for at in tiles(count):
            here = pl.ds(pl.multiple_of(offsets[1] + at.start, at.stop - at.start), at.stop - at.start)
            stat[here, :] = (beta_stat * before[at].astype(f32) + added[at]).astype(bf16)
    squares = jnp.zeros((), f32)
    for at in tiles(stat.shape[0]):
        power = product(stat[at], basis[...])
        iterate[at] = power
        squares += jnp.sum(power * power)
    scale = 1.0 / jnp.sqrt(squares + norm_eps)
    for at in tiles(stat.shape[0]):
        value = iterate[at] * scale
        iterate[at] = value
        half_a[at] = value.astype(bf16)

    def step(source, at):
        gram = product(source[at], source[...], NT).astype(bf16)
        return 1.5 * iterate[at] - 0.5 * product(gram, source[...])

    source, target = half_a, half_b
    for sweep in range(NS_ITERS - 1):
        for at in tiles(stat.shape[0]):
            value = step(source, at)
            iterate[at] = value
            target[at] = value.astype(bf16)
        source, target = target, source
    for place, out in enumerate(outs):
        for at in tiles(out.shape[0]):
            size = at.stop - at.start
            here = pl.ds(pl.multiple_of(offsets[ns + place] + at.start, size), size)
            out[at] = step(source, here).astype(out.dtype)


def build(mesh):
    n_dp, n_tensor, n_section = mesh.shape["dp"], mesh.shape["tensor"], mesh.shape["section"]
    pair = n_dp == 2

    def swap(value):
        return lax.ppermute(value, "dp", [(0, 1), (1, 0)])

    def total(value, axis, count):
        if count & (count - 1):
            return lax.psum(value, axis)
        step = 1
        while step < count:
            value = value + lax.ppermute(value, axis, [(i, i ^ step) for i in range(count)])
            step *= 2
        return value

    def after(value, *others):
        return lax.optimization_barrier((value,) + others)[0]

    def local(
        grad_parts,
        first_moment,
        second_moment,
        left_stat,
        right_stat,
        left_basis,
        right_basis,
        gain_grads,
        gain_first,
        gain_second,
        table_grads,
        table_first,
        table_second,
    ):
        partial_value = grad_parts[0, 0]
        mats, extent, width = partial_value.shape
        rows = left_basis.shape[2]
        dp = lax.axis_index("dp")
        rank = lax.axis_index("tensor")
        own = dp * rows
        other = (n_dp - 1 - dp) * rows

        def columns_of(pieces):
            return [lax.dynamic_slice_in_dim(piece, own, rows, 1) for piece in pieces]

        gain_part = gain_grads[0, 0, 0]
        table_part = table_grads[0, 0]
        both = jnp.concatenate([gain_part.reshape(-1), table_part.reshape(-1)])
        both = total(both, "dp", n_dp)

        if pair:
            section = lax.axis_index("section")
            left_side = (dp == section % 2).astype(jnp.int32)
            left_local = left_basis[0, 0].astype(bf16)
            right_local = right_basis[0, 0].astype(bf16)
            last = None
            blocks = [None] * n_tensor
            for step in reversed(range(n_tensor)):
                mine = lax.dynamic_index_in_dim(partial_value, rank ^ step, 0, keepdims=False)
                sent = lax.dynamic_slice_in_dim(mine, other, rows, 0)
                got = swap(sent)
                if last is None:
                    left_local_out = after(left_local, got)
                else:
                    got = after(got, last)
                block = lax.dynamic_slice_in_dim(mine, own, rows, 0).astype(f32) + got.astype(f32)
                last = block = block.astype(bf16)
                if step:
                    block = lax.ppermute(
                        block, "tensor", [(i, i ^ step) for i in range(n_tensor)]
                    )
                blocks[step] = block
            left_cross_out = lax.dynamic_slice_in_dim(left_local_out, other, rows, 1)
            left_cross = swap(left_cross_out)
            left_rest = lax.ppermute(
                lax.dynamic_slice_in_dim(left_local_out, own, rows, 1),
                ("dp", "section"),
                [
                    ((1 - s % 2) * n_section + s, (s % 2) * n_section + s)
                    for s in range(n_section)
                ],
            )
            right_other = swap(after(right_local, last))
            places = jnp.stack([(rank ^ step) * width for step in range(n_tensor)])
            *blocks, both, left_cross, left_rest = lax.optimization_barrier(
                (*blocks, both, left_cross, left_rest)
            )
            (grad_rows,) = call(
                functools.partial(assemble_kernel, width),
                [shape(rows, extent, bf16)],
                [],
                places,
                *blocks,
            )
            right_pieces = [right_local, right_other]
            (right_full,) = call(
                join_kernel,
                [shape(extent, extent, bf16)],
                [],
                jnp.stack([own, other]),
                *right_pieces,
            )
            grad_other, right_full = lax.optimization_barrier((swap(grad_rows), right_full))
            grad_pieces = [grad_rows, grad_other]
            stat_send = jnp.where(left_side == 1, right_stat[0, 0], left_stat[0, 0]).astype(bf16)
            stat_other = swap(after(stat_send, grad_rows))
            offsets = jnp.stack([own, other])
            left_columns = [lax.dynamic_slice_in_dim(left_local, own, rows, 1), left_cross]
        else:
            columns = lax.all_to_all(partial_value, "tensor", split_axis=0, concat_axis=2, tiled=True)
            summed = lax.psum_scatter(columns, "dp", scatter_dimension=1, tiled=True)
            grad_rows = summed[0]
            left_local = left_basis[0, 0].astype(bf16)
            right_local = right_basis[0, 0].astype(bf16)

            def gather(value):
                return [lax.all_gather(value, "dp", axis=0, tiled=True)]

            grad_pieces, left_pieces, (right_full,) = (
                gather(grad_rows),
                gather(left_local),
                gather(right_local),
            )
            offsets = jnp.zeros((1,), jnp.int32)
            left_columns = columns_of(left_pieces)
        gain_sum = total(both[: gain_part.size].reshape(gain_part.shape), "tensor", n_tensor)
        table_sum = total(both[gain_part.size :].reshape(table_part.shape), "section", n_section)
        grad_pieces[-1], gain_sum, table_sum = lax.optimization_barrier(
            (grad_pieces[-1], gain_sum, table_sum)
        )
        n = len(grad_pieces)
        square = pltpu.VMEM((extent, extent), bf16)
        strip = pltpu.VMEM((extent, rows), bf16)

        first_new, second_new, direction = call(
            functools.partial(moments_kernel, n),
            [shape(rows, extent, f32)] * 2 + [shape(rows, extent, bf16)],
            [square, strip, square],
            offsets,
            *grad_pieces,
            *left_columns,
            right_full,
            first_moment[0, 0],
            second_moment[0, 0],
        )
        direction_pieces = [direction, swap(direction)] if pair else gather(direction)
        grad_rows = after(grad_rows, direction)
        if pair:
            left_new, right_new, stat_keep, stat_added = call(
                pair_stats_kernel,
                [shape(rows, extent, f32)] * 2
                + [shape(rows, extent, bf16), shape(rows, extent, f32)],
                [square],
                jnp.concatenate([offsets, left_side[None]]),
                grad_rows,
                grad_pieces[1],
                left_stat[0, 0],
                right_stat[0, 0],
            )
        else:
            left_new, right_new, left_new_half, right_new_half = call(
                functools.partial(stats_kernel, n),
                [shape(rows, extent, f32)] * 2 + [shape(rows, extent, bf16)] * 2,
                [square, strip],
                offsets,
                *grad_pieces,
                *columns_of(grad_pieces),
                grad_rows,
                left_stat[0, 0],
                right_stat[0, 0],
            )

        def rotation(stat_pieces, basis, outs, bases, *more):
            return call(
                functools.partial(rotation_kernel, len(stat_pieces), len(outs)),
                outs,
                [square, pltpu.VMEM((extent, extent), f32), square, square],
                jnp.concatenate([offsets, jnp.stack(bases)]),
                *stat_pieces,
                basis,
                *more,
            )

        own_rows = shape(rows, extent, f32)
        if pair:
            left_other = jnp.where(
                own < rows,
                jnp.concatenate([left_cross, left_rest], axis=1),
                jnp.concatenate([left_rest, left_cross], axis=1),
            )
            (basis,) = call(
                functools.partial(basis_kernel, n),
                [shape(extent, extent, bf16)],
                [],
                jnp.concatenate([offsets, left_side[None]]),
                left_local,
                left_other,
                right_full,
            )
            basis = after(basis, direction)
            rotation_own, rotation_send = rotation(
                [stat_keep, stat_other],
                basis,
                [own_rows, shape(rows, extent, bf16)],
                [own, other],
                stat_added,
            )
            direction_pieces[1] = after(direction_pieces[1], rotation_send)
            cut = rows * 3 // 4
            rotation_parts = [swap(rotation_send[:cut])]
            rotation_parts.append(swap(rotation_send[cut:]))
        else:
            (left_rotation,) = rotation(gather(left_new_half), left_pieces[0], [own_rows], [own])
            (right_rotation,) = rotation(gather(right_new_half), right_full, [own_rows], [own])
        (update,) = call(
            functools.partial(update_kernel, n),
            [own_rows],
            [square],
            offsets,
            *direction_pieces,
            right_full,
            left_local,
        )
        if pair:
            rotation_parts[0] = after(rotation_parts[0], update)
            left_rotation, right_rotation = place(
                left_side[None], rotation_parts[0], 0, rotation_own, rotation_own
            )
            tail = rotation_parts[1].astype(f32)
            tail_own = rotation_own[cut:]
            left_rotation = left_rotation.at[cut:].set(
                jnp.where(left_side == 1, tail_own, tail)
            )
            right_rotation = right_rotation.at[cut:].set(
                jnp.where(left_side == 1, tail, tail_own)
            )

        gain_moment = beta_first * gain_first[0] + (1.0 - beta_first) * gain_sum
        gain_squares = beta_second * gain_second[0] + (1.0 - beta_second) * gain_sum * gain_sum
        gain_update = adam_direction(gain_moment, gain_squares)
        table_moment = beta_first * table_first + (1.0 - beta_first) * table_sum
        table_squares = beta_second * table_second + (1.0 - beta_second) * table_sum * table_sum
        table_update = adam_direction(table_moment, table_squares)
        return (
            update[None, None],
            first_new[None, None],
            second_new[None, None],
            left_new[None, None],
            right_new[None, None],
            left_rotation[None, None],
            right_rotation[None, None],
            gain_update[None],
            gain_moment[None],
            gain_squares[None],
            table_update,
            table_moment,
            table_squares,
        )

    return local


def solution(mesh):
    state = P("section", "tensor", "dp", None)
    gains = P("section", None, None)
    table = P(None, "tensor")
    return jax.shard_map(
        build(mesh),
        mesh=mesh,
        in_specs=(P("section", "dp", None, None, "tensor"),)
        + (state,) * 6
        + (P("section", "dp", "tensor", None, None), gains, gains)
        + (P("section", "dp", None, "tensor"), table, table),
        out_specs=(state,) * 7 + (gains,) * 3 + (table,) * 3,
        check_vma=False,
    )
```

```python
import functools

import jax
import jax.numpy as jnp
from jax import lax
from jax.experimental import pallas as pl
from jax.experimental.pallas import tpu as pltpu
from jax.sharding import PartitionSpec as P

NS_ITERS = 3

beta_first = 0.9
beta_second = 0.95
beta_stat = 0.95
adam_eps = 1e-08
norm_eps = 1e-06
step_count = 10.0

f32 = jnp.float32
bf16 = jnp.bfloat16
MIB = 1024 * 1024

NN = (((1,), (0,)), ((), ()))
NT = (((1,), (1,)), ((), ()))
TN = (((0,), (0,)), ((), ()))


def product(left, right, dims=NN):
    return lax.dot_general(left, right, dims, preferred_element_type=f32)


def adam_direction(first, second):
    first_hat = first / (1.0 - beta_first**step_count)
    second_hat = second / (1.0 - beta_second**step_count)
    return first_hat / (jnp.sqrt(second_hat) + adam_eps)


def tiles(extent, most=256):
    size = min(extent, most)
    return [slice(start, start + size) for start in range(0, extent, size)]


def join(whole, offsets, pieces):
    for place, piece in enumerate(pieces):
        count = piece.shape[0]
        whole[pl.ds(pl.multiple_of(offsets[place], count), count), :] = piece[...]


def call(kernel, outs, scratch, *operands):
    return pl.pallas_call(
        kernel,
        out_shape=outs,
        in_specs=[pl.BlockSpec(memory_space=pltpu.SMEM)]
        + [pl.BlockSpec(memory_space=pltpu.VMEM)] * (len(operands) - 1),
        out_specs=[pl.BlockSpec(memory_space=pltpu.VMEM)] * len(outs),
        scratch_shapes=scratch,
        compiler_params=pltpu.CompilerParams(vmem_limit_bytes=40 * MIB),
    )(*operands)


def shape(rows, columns, dtype):
    return jax.ShapeDtypeStruct((rows, columns), dtype)


def assemble_kernel(width, places, *refs):
    *blocks, out = refs
    for place, block in enumerate(blocks):
        out[:, pl.ds(pl.multiple_of(places[place], width), width)] = block[...]


def place_kernel(start, side, part, left_in, right_in, left, right, wide, sem):
    del left_in, right_in
    wide[...] = part[...].astype(f32)
    here = pl.ds(start, part.shape[0])

    @pl.when(side[0] == 1)
    def _():
        copy = pltpu.make_async_copy(wide, right.at[here], sem)
        copy.start()
        copy.wait()

    @pl.when(side[0] != 1)
    def _():
        copy = pltpu.make_async_copy(wide, left.at[here], sem)
        copy.start()
        copy.wait()


def place(side, part, start, left, right):
    anywhere = pl.BlockSpec(memory_space=pl.ANY)
    return pl.pallas_call(
        functools.partial(place_kernel, start),
        out_shape=[shape(*left.shape, f32)] * 2,
        in_specs=[
            pl.BlockSpec(memory_space=pltpu.SMEM),
            pl.BlockSpec(memory_space=pltpu.VMEM),
            anywhere,
            anywhere,
        ],
        out_specs=[anywhere, anywhere],
        scratch_shapes=[pltpu.VMEM(part.shape, f32), pltpu.SemaphoreType.DMA],
        input_output_aliases={2: 0, 3: 1},
    )(side, part, left, right)


def join_kernel(offsets, *refs):
    *pieces, out = refs
    join(out, offsets, pieces)


def basis_kernel(n, scalars, *refs):
    *left_pieces, right, out = refs
    left_side = scalars[n] == 1

    @pl.when(left_side)
    def _():
        join(out, scalars, left_pieces)

    @pl.when(jnp.logical_not(left_side))
    def _():
        out[...] = right[...]


def stats_kernel(n, offsets, *refs):
    pieces, column_pieces = refs[:n], refs[n : 2 * n]
    rows_ref, left_stat, right_stat = refs[2 * n : 2 * n + 3]
    left_next, right_next, left_half, right_half, grad, columns = refs[2 * n + 3 :]
    join(grad, offsets, pieces)
    join(columns, offsets, column_pieces)
    for at in tiles(rows_ref.shape[0]):
        left_new = beta_stat * left_stat[at] + product(rows_ref[at], grad[...], NT)
        right_new = beta_stat * right_stat[at] + product(columns[:, at], grad[...], TN)
        left_next[at] = left_new
        right_next[at] = right_new
        left_half[at] = left_new.astype(bf16)
        right_half[at] = right_new.astype(bf16)


def pair_stats_kernel(offsets, *refs):
    (own_rows, other_rows), left_stat, right_stat = refs[:2], refs[2], refs[3]
    left_next, right_next, keep, added, grad = refs[4:]
    join(grad, offsets, (own_rows, other_rows))
    count = own_rows.shape[0]
    own = pl.multiple_of(offsets[0], count)
    other = pl.multiple_of(offsets[1], count)
    for at in tiles(count):
        columns = grad[:, pl.ds(own + at.start, at.stop - at.start)]
        left_next[at] = beta_stat * left_stat[at] + product(own_rows[at], grad[...], NT)
        right_next[at] = beta_stat * right_stat[at] + product(columns, grad[...], TN)
    left_side = offsets[2] == 1

    @pl.when(left_side)
    def _():
        keep[...] = left_next[...].astype(bf16)
        for at in tiles(count):
            added[at] = product(other_rows[at], grad[...], NT)

    @pl.when(jnp.logical_not(left_side))
    def _():
        keep[...] = right_next[...].astype(bf16)
        for at in tiles(count):
            columns = grad[:, pl.ds(other + at.start, at.stop - at.start)]
            added[at] = product(columns, grad[...], TN)


def moments_kernel(n, offsets, *refs):
    pieces, column_pieces, right = refs[:n], refs[n : 2 * n], refs[2 * n]
    first, second = refs[2 * n + 1 : 2 * n + 3]
    first_next, second_next, direction, grad, columns, rotated_half = refs[2 * n + 3 :]
    join(grad, offsets, pieces)
    join(columns, offsets, column_pieces)
    for at in tiles(grad.shape[0]):
        rotated_half[at] = product(grad[at], right[...]).astype(bf16)
    for at in tiles(first.shape[0]):
        rotated = product(columns[:, at], rotated_half[...], TN)
        first_new = beta_first * first[at] + (1.0 - beta_first) * rotated
        second_new = beta_second * second[at] + (1.0 - beta_second) * rotated * rotated
        first_next[at] = first_new
        second_next[at] = second_new
        direction[at] = adam_direction(first_new, second_new).astype(bf16)


def update_kernel(n, offsets, *refs):
    pieces, right, rows_ref, update, direction = refs[:n], *refs[n:]
    join(direction, offsets, pieces)
    for at in tiles(rows_ref.shape[0]):
        back_half = product(rows_ref[at], direction[...]).astype(bf16)
        update[at] = product(back_half, right[...], NT)


def rotation_kernel(ns, n_out, offsets, *refs):
    stat_pieces, basis, outs = refs[:ns], refs[ns], refs[-4 - n_out : -4]
    stat, iterate, half_a, half_b = refs[-4:]
    join(stat, offsets, stat_pieces[:1])
    if ns > 1:
        before, added = stat_pieces[1], refs[ns + 1]
        count = before.shape[0]
        for at in tiles(count):
            here = pl.ds(pl.multiple_of(offsets[1] + at.start, at.stop - at.start), at.stop - at.start)
            stat[here, :] = (beta_stat * before[at].astype(f32) + added[at]).astype(bf16)
    squares = jnp.zeros((), f32)
    for at in tiles(stat.shape[0]):
        power = product(stat[at], basis[...])
        iterate[at] = power
        squares += jnp.sum(power * power)
    scale = 1.0 / jnp.sqrt(squares + norm_eps)
    for at in tiles(stat.shape[0]):
        value = iterate[at] * scale
        iterate[at] = value
        half_a[at] = value.astype(bf16)

    def step(source, at):
        gram = product(source[at], source[...], NT).astype(bf16)
        return 1.5 * iterate[at] - 0.5 * product(gram, source[...])

    source, target = half_a, half_b
    for sweep in range(NS_ITERS - 1):
        for at in tiles(stat.shape[0]):
            value = step(source, at)
            iterate[at] = value
            target[at] = value.astype(bf16)
        source, target = target, source
    for place, out in enumerate(outs):
        for at in tiles(out.shape[0]):
            size = at.stop - at.start
            here = pl.ds(pl.multiple_of(offsets[ns + place] + at.start, size), size)
            out[at] = step(source, here).astype(out.dtype)


def build(mesh):
    n_dp, n_tensor, n_section = mesh.shape["dp"], mesh.shape["tensor"], mesh.shape["section"]
    pair = n_dp == 2

    def swap(value):
        return lax.ppermute(value, "dp", [(0, 1), (1, 0)])

    def total(value, axis, count):
        if count & (count - 1):
            return lax.psum(value, axis)
        step = 1
        while step < count:
            value = value + lax.ppermute(value, axis, [(i, i ^ step) for i in range(count)])
            step *= 2
        return value

    def after(value, *others):
        return lax.optimization_barrier((value,) + others)[0]

    def local(
        grad_parts,
        first_moment,
        second_moment,
        left_stat,
        right_stat,
        left_basis,
        right_basis,
        gain_grads,
        gain_first,
        gain_second,
        table_grads,
        table_first,
        table_second,
    ):
        partial_value = grad_parts[0, 0]
        mats, extent, width = partial_value.shape
        rows = left_basis.shape[2]
        dp = lax.axis_index("dp")
        rank = lax.axis_index("tensor")
        own = dp * rows
        other = (n_dp - 1 - dp) * rows

        def columns_of(pieces):
            return [lax.dynamic_slice_in_dim(piece, own, rows, 1) for piece in pieces]

        gain_part = gain_grads[0, 0, 0]
        table_part = table_grads[0, 0]
        both = jnp.concatenate([gain_part.reshape(-1), table_part.reshape(-1)])
        both = total(both, "dp", n_dp)

        if pair:
            section = lax.axis_index("section")
            left_side = (dp == section % 2).astype(jnp.int32)
            left_local = left_basis[0, 0].astype(bf16)
            right_local = right_basis[0, 0].astype(bf16)
            last = None
            to_send = partial_value
            blocks = [None] * n_tensor
            for step in reversed(range(n_tensor)):
                mine = lax.dynamic_index_in_dim(partial_value, rank ^ step, 0, keepdims=False)
                sent = lax.dynamic_slice_in_dim(
                    lax.dynamic_index_in_dim(to_send, rank ^ step, 0, keepdims=False),
                    other,
                    rows,
                    0,
                )
                got = swap(sent)
                if last is None:
                    to_send = after(to_send, sent)
                    left_local_out = after(left_local, got)
                else:
                    got = after(got, last)
                block = lax.dynamic_slice_in_dim(mine, own, rows, 0).astype(f32) + got.astype(f32)
                last = block = block.astype(bf16)
                if step:
                    block = lax.ppermute(
                        block, "tensor", [(i, i ^ step) for i in range(n_tensor)]
                    )
                blocks[step] = block
            left_cross_out = lax.dynamic_slice_in_dim(left_local_out, other, rows, 1)
            left_cross = swap(left_cross_out)
            left_rest = lax.ppermute(
                lax.dynamic_slice_in_dim(left_local_out, own, rows, 1),
                ("dp", "section"),
                [
                    ((1 - s % 2) * n_section + s, (s % 2) * n_section + s)
                    for s in range(n_section)
                ],
            )
            right_other = swap(after(right_local, last))
            places = jnp.stack([(rank ^ step) * width for step in range(n_tensor)])
            *blocks, both, left_cross, left_rest = lax.optimization_barrier(
                (*blocks, both, left_cross, left_rest)
            )
            (grad_rows,) = call(
                functools.partial(assemble_kernel, width),
                [shape(rows, extent, bf16)],
                [],
                places,
                *blocks,
            )
            right_pieces = [right_local, right_other]
            (right_full,) = call(
                join_kernel,
                [shape(extent, extent, bf16)],
                [],
                jnp.stack([own, other]),
                *right_pieces,
            )
            grad_other, right_full = lax.optimization_barrier((swap(grad_rows), right_full))
            grad_pieces = [grad_rows, grad_other]
            stat_send = jnp.where(left_side == 1, right_stat[0, 0], left_stat[0, 0]).astype(bf16)
            stat_other = swap(after(stat_send, grad_rows))
            offsets = jnp.stack([own, other])
            left_columns = [lax.dynamic_slice_in_dim(left_local, own, rows, 1), left_cross]
        else:
            columns = lax.all_to_all(partial_value, "tensor", split_axis=0, concat_axis=2, tiled=True)
            summed = lax.psum_scatter(columns, "dp", scatter_dimension=1, tiled=True)
            grad_rows = summed[0]
            left_local = left_basis[0, 0].astype(bf16)
            right_local = right_basis[0, 0].astype(bf16)

            def gather(value):
                return [lax.all_gather(value, "dp", axis=0, tiled=True)]

            grad_pieces, left_pieces, (right_full,) = (
                gather(grad_rows),
                gather(left_local),
                gather(right_local),
            )
            offsets = jnp.zeros((1,), jnp.int32)
            left_columns = columns_of(left_pieces)
        gain_sum = total(both[: gain_part.size].reshape(gain_part.shape), "tensor", n_tensor)
        table_sum = total(both[gain_part.size :].reshape(table_part.shape), "section", n_section)
        grad_pieces[-1], gain_sum, table_sum = lax.optimization_barrier(
            (grad_pieces[-1], gain_sum, table_sum)
        )
        n = len(grad_pieces)
        square = pltpu.VMEM((extent, extent), bf16)
        strip = pltpu.VMEM((extent, rows), bf16)

        first_new, second_new, direction = call(
            functools.partial(moments_kernel, n),
            [shape(rows, extent, f32)] * 2 + [shape(rows, extent, bf16)],
            [square, strip, square],
            offsets,
            *grad_pieces,
            *left_columns,
            right_full,
            first_moment[0, 0],
            second_moment[0, 0],
        )
        direction_pieces = [direction, swap(direction)] if pair else gather(direction)
        grad_rows = after(grad_rows, direction)
        if pair:
            left_new, right_new, stat_keep, stat_added = call(
                pair_stats_kernel,
                [shape(rows, extent, f32)] * 2
                + [shape(rows, extent, bf16), shape(rows, extent, f32)],
                [square],
                jnp.concatenate([offsets, left_side[None]]),
                grad_rows,
                grad_pieces[1],
                left_stat[0, 0],
                right_stat[0, 0],
            )
        else:
            left_new, right_new, left_new_half, right_new_half = call(
                functools.partial(stats_kernel, n),
                [shape(rows, extent, f32)] * 2 + [shape(rows, extent, bf16)] * 2,
                [square, strip],
                offsets,
                *grad_pieces,
                *columns_of(grad_pieces),
                grad_rows,
                left_stat[0, 0],
                right_stat[0, 0],
            )

        def rotation(stat_pieces, basis, outs, bases, *more):
            return call(
                functools.partial(rotation_kernel, len(stat_pieces), len(outs)),
                outs,
                [square, pltpu.VMEM((extent, extent), f32), square, square],
                jnp.concatenate([offsets, jnp.stack(bases)]),
                *stat_pieces,
                basis,
                *more,
            )

        own_rows = shape(rows, extent, f32)
        if pair:
            left_other = jnp.where(
                own < rows,
                jnp.concatenate([left_cross, left_rest], axis=1),
                jnp.concatenate([left_rest, left_cross], axis=1),
            )
            (basis,) = call(
                functools.partial(basis_kernel, n),
                [shape(extent, extent, bf16)],
                [],
                jnp.concatenate([offsets, left_side[None]]),
                left_local,
                left_other,
                right_full,
            )
            basis = after(basis, direction)
            rotation_own, rotation_send = rotation(
                [stat_keep, stat_other],
                basis,
                [own_rows, shape(rows, extent, bf16)],
                [own, other],
                stat_added,
            )
            direction_pieces[1] = after(direction_pieces[1], rotation_send)
            cut = rows * 3 // 4
            rotation_parts = [swap(rotation_send[:cut])]
            rotation_parts.append(swap(rotation_send[cut:]))
        else:
            (left_rotation,) = rotation(gather(left_new_half), left_pieces[0], [own_rows], [own])
            (right_rotation,) = rotation(gather(right_new_half), right_full, [own_rows], [own])
        (update,) = call(
            functools.partial(update_kernel, n),
            [own_rows],
            [square],
            offsets,
            *direction_pieces,
            right_full,
            left_local,
        )
        if pair:
            rotation_parts[0] = after(rotation_parts[0], update)
            left_rotation, right_rotation = place(
                left_side[None], rotation_parts[0], 0, rotation_own, rotation_own
            )
            tail = rotation_parts[1].astype(f32)
            tail_own = rotation_own[cut:]
            left_rotation = left_rotation.at[cut:].set(
                jnp.where(left_side == 1, tail_own, tail)
            )
            right_rotation = right_rotation.at[cut:].set(
                jnp.where(left_side == 1, tail, tail_own)
            )

        gain_moment = beta_first * gain_first[0] + (1.0 - beta_first) * gain_sum
        gain_squares = beta_second * gain_second[0] + (1.0 - beta_second) * gain_sum * gain_sum
        gain_update = adam_direction(gain_moment, gain_squares)
        table_moment = beta_first * table_first + (1.0 - beta_first) * table_sum
        table_squares = beta_second * table_second + (1.0 - beta_second) * table_sum * table_sum
        table_update = adam_direction(table_moment, table_squares)
        return (
            update[None, None],
            first_new[None, None],
            second_new[None, None],
            left_new[None, None],
            right_new[None, None],
            left_rotation[None, None],
            right_rotation[None, None],
            gain_update[None],
            gain_moment[None],
            gain_squares[None],
            table_update,
            table_moment,
            table_squares,
        )

    return local


def solution(mesh):
    state = P("section", "tensor", "dp", None)
    gains = P("section", None, None)
    table = P(None, "tensor")
    return jax.shard_map(
        build(mesh),
        mesh=mesh,
        in_specs=(P("section", "dp", None, None, "tensor"),)
        + (state,) * 6
        + (P("section", "dp", "tensor", None, None), gains, gains)
        + (P("section", "dp", None, "tensor"), table, table),
        out_specs=(state,) * 7 + (gains,) * 3 + (table,) * 3,
        check_vma=False,
    )
```

```python
import functools

import jax
import jax.numpy as jnp
from jax import lax
from jax.experimental import pallas as pl
from jax.experimental.pallas import tpu as pltpu
from jax.sharding import PartitionSpec as P

NS_ITERS = 3

beta_first = 0.9
beta_second = 0.95
beta_stat = 0.95
adam_eps = 1e-08
norm_eps = 1e-06
step_count = 10.0

f32 = jnp.float32
bf16 = jnp.bfloat16
MIB = 1024 * 1024

NN = (((1,), (0,)), ((), ()))
NT = (((1,), (1,)), ((), ()))
TN = (((0,), (0,)), ((), ()))


def product(left, right, dims=NN):
    return lax.dot_general(left, right, dims, preferred_element_type=f32)


def adam_direction(first, second):
    first_hat = first / (1.0 - beta_first**step_count)
    second_hat = second / (1.0 - beta_second**step_count)
    return first_hat / (jnp.sqrt(second_hat) + adam_eps)


def tiles(extent, most=256):
    size = min(extent, most)
    return [slice(start, start + size) for start in range(0, extent, size)]


def join(whole, offsets, pieces):
    for place, piece in enumerate(pieces):
        count = piece.shape[0]
        whole[pl.ds(pl.multiple_of(offsets[place], count), count), :] = piece[...]


def call(kernel, outs, scratch, *operands):
    return pl.pallas_call(
        kernel,
        out_shape=outs,
        in_specs=[pl.BlockSpec(memory_space=pltpu.SMEM)]
        + [pl.BlockSpec(memory_space=pltpu.VMEM)] * (len(operands) - 1),
        out_specs=[pl.BlockSpec(memory_space=pltpu.VMEM)] * len(outs),
        scratch_shapes=scratch,
        compiler_params=pltpu.CompilerParams(vmem_limit_bytes=40 * MIB),
    )(*operands)


def shape(rows, columns, dtype):
    return jax.ShapeDtypeStruct((rows, columns), dtype)


def assemble_kernel(width, places, *refs):
    *blocks, out = refs
    for place, block in enumerate(blocks):
        out[:, pl.ds(pl.multiple_of(places[place], width), width)] = block[...]


def place_kernel(start, side, part, left_in, right_in, left, right, wide, sem):
    del left_in, right_in
    wide[...] = part[...].astype(f32)
    here = pl.ds(start, part.shape[0])

    @pl.when(side[0] == 1)
    def _():
        copy = pltpu.make_async_copy(wide, right.at[here], sem)
        copy.start()
        copy.wait()

    @pl.when(side[0] != 1)
    def _():
        copy = pltpu.make_async_copy(wide, left.at[here], sem)
        copy.start()
        copy.wait()


def place(side, part, start, left, right):
    anywhere = pl.BlockSpec(memory_space=pl.ANY)
    return pl.pallas_call(
        functools.partial(place_kernel, start),
        out_shape=[shape(*left.shape, f32)] * 2,
        in_specs=[
            pl.BlockSpec(memory_space=pltpu.SMEM),
            pl.BlockSpec(memory_space=pltpu.VMEM),
            anywhere,
            anywhere,
        ],
        out_specs=[anywhere, anywhere],
        scratch_shapes=[pltpu.VMEM(part.shape, f32), pltpu.SemaphoreType.DMA],
        input_output_aliases={2: 0, 3: 1},
    )(side, part, left, right)


def join_kernel(offsets, *refs):
    *pieces, out = refs
    join(out, offsets, pieces)


def basis_kernel(n, scalars, *refs):
    *left_pieces, right, out = refs
    left_side = scalars[n] == 1

    @pl.when(left_side)
    def _():
        join(out, scalars, left_pieces)

    @pl.when(jnp.logical_not(left_side))
    def _():
        out[...] = right[...]


def stats_kernel(n, offsets, *refs):
    pieces, column_pieces = refs[:n], refs[n : 2 * n]
    rows_ref, left_stat, right_stat = refs[2 * n : 2 * n + 3]
    left_next, right_next, left_half, right_half, grad, columns = refs[2 * n + 3 :]
    join(grad, offsets, pieces)
    join(columns, offsets, column_pieces)
    for at in tiles(rows_ref.shape[0]):
        left_new = beta_stat * left_stat[at] + product(rows_ref[at], grad[...], NT)
        right_new = beta_stat * right_stat[at] + product(columns[:, at], grad[...], TN)
        left_next[at] = left_new
        right_next[at] = right_new
        left_half[at] = left_new.astype(bf16)
        right_half[at] = right_new.astype(bf16)


def pair_stats_kernel(offsets, *refs):
    (own_rows, other_rows), left_stat, right_stat = refs[:2], refs[2], refs[3]
    left_next, right_next, keep, added, grad = refs[4:]
    join(grad, offsets, (own_rows, other_rows))
    count = own_rows.shape[0]
    own = pl.multiple_of(offsets[0], count)
    other = pl.multiple_of(offsets[1], count)
    for at in tiles(count):
        columns = grad[:, pl.ds(own + at.start, at.stop - at.start)]
        left_next[at] = beta_stat * left_stat[at] + product(own_rows[at], grad[...], NT)
        right_next[at] = beta_stat * right_stat[at] + product(columns, grad[...], TN)
    left_side = offsets[2] == 1

    @pl.when(left_side)
    def _():
        keep[...] = left_next[...].astype(bf16)
        for at in tiles(count):
            added[at] = product(other_rows[at], grad[...], NT)

    @pl.when(jnp.logical_not(left_side))
    def _():
        keep[...] = right_next[...].astype(bf16)
        for at in tiles(count):
            columns = grad[:, pl.ds(other + at.start, at.stop - at.start)]
            added[at] = product(columns, grad[...], TN)


def moments_kernel(n, offsets, *refs):
    pieces, column_pieces, right = refs[:n], refs[n : 2 * n], refs[2 * n]
    first, second = refs[2 * n + 1 : 2 * n + 3]
    first_next, second_next, direction, grad, columns, rotated_half = refs[2 * n + 3 :]
    join(grad, offsets, pieces)
    join(columns, offsets, column_pieces)
    for at in tiles(grad.shape[0]):
        rotated_half[at] = product(grad[at], right[...]).astype(bf16)
    for at in tiles(first.shape[0]):
        rotated = product(columns[:, at], rotated_half[...], TN)
        first_new = beta_first * first[at] + (1.0 - beta_first) * rotated
        second_new = beta_second * second[at] + (1.0 - beta_second) * rotated * rotated
        first_next[at] = first_new
        second_next[at] = second_new
        direction[at] = adam_direction(first_new, second_new).astype(bf16)


def update_kernel(n, offsets, *refs):
    pieces, right, rows_ref, update, direction = refs[:n], *refs[n:]
    join(direction, offsets, pieces)
    for at in tiles(rows_ref.shape[0]):
        back_half = product(rows_ref[at], direction[...]).astype(bf16)
        update[at] = product(back_half, right[...], NT)


def rotation_kernel(ns, n_out, offsets, *refs):
    stat_pieces, basis, outs = refs[:ns], refs[ns], refs[-4 - n_out : -4]
    stat, iterate, half_a, half_b = refs[-4:]
    join(stat, offsets, stat_pieces[:1])
    if ns > 1:
        before, added = stat_pieces[1], refs[ns + 1]
        count = before.shape[0]
        for at in tiles(count):
            here = pl.ds(pl.multiple_of(offsets[1] + at.start, at.stop - at.start), at.stop - at.start)
            stat[here, :] = (beta_stat * before[at].astype(f32) + added[at]).astype(bf16)
    squares = jnp.zeros((), f32)
    for at in tiles(stat.shape[0]):
        power = product(stat[at], basis[...])
        iterate[at] = power
        squares += jnp.sum(power * power)
    scale = 1.0 / jnp.sqrt(squares + norm_eps)
    for at in tiles(stat.shape[0]):
        value = iterate[at] * scale
        iterate[at] = value
        half_a[at] = value.astype(bf16)

    def step(source, at):
        gram = product(source[at], source[...], NT).astype(bf16)
        return 1.5 * iterate[at] - 0.5 * product(gram, source[...])

    source, target = half_a, half_b
    for sweep in range(NS_ITERS - 1):
        for at in tiles(stat.shape[0]):
            value = step(source, at)
            iterate[at] = value
            target[at] = value.astype(bf16)
        source, target = target, source
    for place, out in enumerate(outs):
        for at in tiles(out.shape[0]):
            size = at.stop - at.start
            here = pl.ds(pl.multiple_of(offsets[ns + place] + at.start, size), size)
            out[at] = step(source, here).astype(out.dtype)


def build(mesh):
    n_dp, n_tensor, n_section = mesh.shape["dp"], mesh.shape["tensor"], mesh.shape["section"]
    pair = n_dp == 2

    def swap(value):
        return lax.ppermute(value, "dp", [(0, 1), (1, 0)])

    def total(value, axis, count):
        if count & (count - 1):
            return lax.psum(value, axis)
        step = 1
        while step < count:
            value = value + lax.ppermute(value, axis, [(i, i ^ step) for i in range(count)])
            step *= 2
        return value

    def after(value, *others):
        return lax.optimization_barrier((value,) + others)[0]

    def local(
        grad_parts,
        first_moment,
        second_moment,
        left_stat,
        right_stat,
        left_basis,
        right_basis,
        gain_grads,
        gain_first,
        gain_second,
        table_grads,
        table_first,
        table_second,
    ):
        partial_value = grad_parts[0, 0]
        mats, extent, width = partial_value.shape
        rows = left_basis.shape[2]
        dp = lax.axis_index("dp")
        rank = lax.axis_index("tensor")
        own = dp * rows
        other = (n_dp - 1 - dp) * rows

        def columns_of(pieces):
            return [lax.dynamic_slice_in_dim(piece, own, rows, 1) for piece in pieces]

        gain_part = gain_grads[0, 0, 0]
        table_part = table_grads[0, 0]
        both = jnp.concatenate([gain_part.reshape(-1), table_part.reshape(-1)])
        both = total(both, "dp", n_dp)

        if pair:
            section = lax.axis_index("section")
            left_side = (dp == section % 2).astype(jnp.int32)
            left_local = left_basis[0, 0].astype(bf16)
            right_local = right_basis[0, 0].astype(bf16)
            last = None
            to_send = partial_value
            blocks = [None] * n_tensor
            for step in reversed(range(n_tensor)):
                mine = lax.dynamic_index_in_dim(partial_value, rank ^ step, 0, keepdims=False)
                sent = lax.dynamic_slice_in_dim(
                    lax.dynamic_index_in_dim(to_send, rank ^ step, 0, keepdims=False),
                    other,
                    rows,
                    0,
                )
                got = swap(sent)
                if last is None:
                    to_send = after(to_send, sent)
                    left_local_out = after(left_local, got)
                else:
                    got = after(got, last)
                block = lax.dynamic_slice_in_dim(mine, own, rows, 0).astype(f32) + got.astype(f32)
                last = block = block.astype(bf16)
                if step:
                    block = lax.ppermute(
                        block, "tensor", [(i, i ^ step) for i in range(n_tensor)]
                    )
                blocks[step] = block
            left_cross_out = lax.dynamic_slice_in_dim(left_local_out, other, rows, 1)
            left_cross = swap(left_cross_out)
            left_rest = lax.ppermute(
                lax.dynamic_slice_in_dim(left_local_out, own, rows, 1),
                ("dp", "section"),
                [
                    ((1 - s % 2) * n_section + s, (s % 2) * n_section + s)
                    for s in range(n_section)
                ],
            )
            right_other = swap(after(right_local, last))
            places = jnp.stack([(rank ^ step) * width for step in range(n_tensor)])
            *blocks, both, left_cross, left_rest = lax.optimization_barrier(
                (*blocks, both, left_cross, left_rest)
            )
            (grad_rows,) = call(
                functools.partial(assemble_kernel, width),
                [shape(rows, extent, bf16)],
                [],
                places,
                *blocks,
            )
            right_pieces = [right_local, right_other]
            (right_full,) = call(
                join_kernel,
                [shape(extent, extent, bf16)],
                [],
                jnp.stack([own, other]),
                *right_pieces,
            )
            grad_other, right_full = lax.optimization_barrier((swap(grad_rows), right_full))
            grad_pieces = [grad_rows, grad_other]
            stat_send = jnp.where(left_side == 1, right_stat[0, 0], left_stat[0, 0]).astype(bf16)
            stat_other = swap(after(stat_send, grad_rows))
            offsets = jnp.stack([own, other])
            left_columns = [lax.dynamic_slice_in_dim(left_local, own, rows, 1), left_cross]
        else:
            columns = lax.all_to_all(partial_value, "tensor", split_axis=0, concat_axis=2, tiled=True)
            summed = lax.psum_scatter(columns, "dp", scatter_dimension=1, tiled=True)
            grad_rows = summed[0]
            left_local = left_basis[0, 0].astype(bf16)
            right_local = right_basis[0, 0].astype(bf16)

            def gather(value):
                return [lax.all_gather(value, "dp", axis=0, tiled=True)]

            grad_pieces, left_pieces, (right_full,) = (
                gather(grad_rows),
                gather(left_local),
                gather(right_local),
            )
            offsets = jnp.zeros((1,), jnp.int32)
            left_columns = columns_of(left_pieces)
        gain_sum = total(both[: gain_part.size].reshape(gain_part.shape), "tensor", n_tensor)
        table_sum = total(both[gain_part.size :].reshape(table_part.shape), "section", n_section)
        grad_pieces[-1], gain_sum, table_sum = lax.optimization_barrier(
            (grad_pieces[-1], gain_sum, table_sum)
        )
        n = len(grad_pieces)
        square = pltpu.VMEM((extent, extent), bf16)
        strip = pltpu.VMEM((extent, rows), bf16)

        first_new, second_new, direction = call(
            functools.partial(moments_kernel, n),
            [shape(rows, extent, f32)] * 2 + [shape(rows, extent, bf16)],
            [square, strip, square],
            offsets,
            *grad_pieces,
            *left_columns,
            right_full,
            first_moment[0, 0],
            second_moment[0, 0],
        )
        direction_pieces = [direction, swap(direction)] if pair else gather(direction)
        grad_rows = after(grad_rows, direction)
        if pair:
            left_new, right_new, stat_keep, stat_added = call(
                pair_stats_kernel,
                [shape(rows, extent, f32)] * 2
                + [shape(rows, extent, bf16), shape(rows, extent, f32)],
                [square],
                jnp.concatenate([offsets, left_side[None]]),
                grad_rows,
                grad_pieces[1],
                left_stat[0, 0],
                right_stat[0, 0],
            )
        else:
            left_new, right_new, left_new_half, right_new_half = call(
                functools.partial(stats_kernel, n),
                [shape(rows, extent, f32)] * 2 + [shape(rows, extent, bf16)] * 2,
                [square, strip],
                offsets,
                *grad_pieces,
                *columns_of(grad_pieces),
                grad_rows,
                left_stat[0, 0],
                right_stat[0, 0],
            )

        def rotation(stat_pieces, basis, outs, bases, *more):
            return call(
                functools.partial(rotation_kernel, len(stat_pieces), len(outs)),
                outs,
                [square, pltpu.VMEM((extent, extent), f32), square, square],
                jnp.concatenate([offsets, jnp.stack(bases)]),
                *stat_pieces,
                basis,
                *more,
            )

        own_rows = shape(rows, extent, f32)
        if pair:
            left_other = jnp.where(
                own < rows,
                jnp.concatenate([left_cross, left_rest], axis=1),
                jnp.concatenate([left_rest, left_cross], axis=1),
            )
            (basis,) = call(
                functools.partial(basis_kernel, n),
                [shape(extent, extent, bf16)],
                [],
                jnp.concatenate([offsets, left_side[None]]),
                left_local,
                left_other,
                right_full,
            )
            basis = after(basis, direction)
            rotation_own, rotation_send = rotation(
                [stat_keep, stat_other],
                basis,
                [own_rows, shape(rows, extent, bf16)],
                [own, other],
                stat_added,
            )
            direction_pieces[1] = after(direction_pieces[1], rotation_send)
            cut = rows * 13 // 16
            rotation_parts = [swap(rotation_send[:cut])]
            rotation_parts.append(swap(rotation_send[cut:]))
        else:
            (left_rotation,) = rotation(gather(left_new_half), left_pieces[0], [own_rows], [own])
            (right_rotation,) = rotation(gather(right_new_half), right_full, [own_rows], [own])
        (update,) = call(
            functools.partial(update_kernel, n),
            [own_rows],
            [square],
            offsets,
            *direction_pieces,
            right_full,
            left_local,
        )
        if pair:
            rotation_parts[0] = after(rotation_parts[0], update)
            left_rotation, right_rotation = place(
                left_side[None], rotation_parts[0], 0, rotation_own, rotation_own
            )
            tail = rotation_parts[1].astype(f32)
            tail_own = rotation_own[cut:]
            left_rotation = left_rotation.at[cut:].set(
                jnp.where(left_side == 1, tail_own, tail)
            )
            right_rotation = right_rotation.at[cut:].set(
                jnp.where(left_side == 1, tail, tail_own)
            )

        gain_moment = beta_first * gain_first[0] + (1.0 - beta_first) * gain_sum
        gain_squares = beta_second * gain_second[0] + (1.0 - beta_second) * gain_sum * gain_sum
        gain_update = adam_direction(gain_moment, gain_squares)
        table_moment = beta_first * table_first + (1.0 - beta_first) * table_sum
        table_squares = beta_second * table_second + (1.0 - beta_second) * table_sum * table_sum
        table_update = adam_direction(table_moment, table_squares)
        return (
            update[None, None],
            first_new[None, None],
            second_new[None, None],
            left_new[None, None],
            right_new[None, None],
            left_rotation[None, None],
            right_rotation[None, None],
            gain_update[None],
            gain_moment[None],
            gain_squares[None],
            table_update,
            table_moment,
            table_squares,
        )

    return local


def solution(mesh):
    state = P("section", "tensor", "dp", None)
    gains = P("section", None, None)
    table = P(None, "tensor")
    return jax.shard_map(
        build(mesh),
        mesh=mesh,
        in_specs=(P("section", "dp", None, None, "tensor"),)
        + (state,) * 6
        + (P("section", "dp", "tensor", None, None), gains, gains)
        + (P("section", "dp", None, "tensor"), table, table),
        out_specs=(state,) * 7 + (gains,) * 3 + (table,) * 3,
        check_vma=False,
    )
```
